512 devices in a mesh: memory: 16 (over z), group: 32 (over y, x, core).
Axes of the slice: x: 4, y: 4, z: 16, core: 2. Of those that a mesh axis runs over, the one named last changes fastest.
Arguments:
- queries: bfloat16 [32, 128, 32, 128], P('group', 'memory')
- positives: bfloat16 [32, 128, 128, 128], P('group', 'memory'), may hold values from -6 to 6
- memory: bfloat16 [32, 2048, 128, 128], P('group', 'memory'), may hold values from -6 to 6
- candidates: int32 [32, 128, 64], P('group', 'memory'), may hold values from 0 to 2047, as said below
- counts: int32 [32, 128], P('group', 'memory'), may hold values from 16 to 32
Outputs:
- batch_scores: float32 [32, 128, 256], P('group', 'memory')
- memory_scores: float32 [32, 128, 64], P('group', 'memory')
- loss: float32 [32, 128], P('group', 'memory')
The draws below stay inside these ranges and needn't reach their ends.
Inputs may be any that keep to these rules, and one draw needn't show every extreme that they name: `candidates`: passage id r of a column lies on memory index r // 128. Among the valid slots of the queries of one device (queries[g, m * 8 to (m + 1) * 8 - 1]), at most 24 name passages of any one memory index, and some memory index is named by exactly 24 of them. Ids may repeat.
All inputs are finite; a program needn't handle non-finite values.
Results may differ from the reference program's by a relative error of at most 0.0003.
Values may be sent and summed in bfloat16 or wider, within the bound.
A program may use at most 128 MiB of HBM per device.

```python
import jax
import jax.numpy as jnp
from jax import lax

D = 128
QT = 32
S = 128
C = 64
Q_DEV = 8
P_DEV = 128
GROUPS = 32
Q_COL = 128
P_COL = 2048
CAP = 24
N_GROUP = 32


def draw_queries(key, part):
    values = jax.random.normal(key, (GROUPS, Q_COL, QT, D), jnp.float32) * D ** (-0.5)
    return values.astype(jnp.bfloat16)


def block_ids(key):
    shards = P_COL // P_DEV
    total = Q_DEV * C
    live = C // 2 * Q_DEV - CAP
    first, second, third, fourth = jax.random.split(key, 4)
    hottest = jax.random.randint(first, (), 0, shards)
    shuffled = jax.random.permutation(second, live).astype(jnp.int32)
    offsets = jnp.concatenate([jnp.zeros((CAP,), jnp.int32), 1 + shuffled % (shards - 1), jax.random.randint(third, (total - CAP - live,), 1, shards)])
    owners = (hottest + offsets) % shards
    local_rows = jax.random.randint(fourth, (total,), 0, P_DEV)
    ids = owners * P_DEV + local_rows
    return ids.reshape(C, Q_DEV).T


def draw_candidates(key, part):
    keys = jax.random.split(key, GROUPS * (Q_COL // Q_DEV))
    blocks = jax.vmap(block_ids)(keys)
    return blocks.reshape(GROUPS, Q_COL, C).astype(jnp.int32)


def place_ends(drawn, stream_key, smallest, top_value):
    spot = [jax.random.randint(jax.random.fold_in(stream_key, axis), (), 0, length) for axis, length in enumerate(drawn.shape)]
    longest = drawn.shape.index(max(drawn.shape))
    neighbour = spot[:longest] + [(spot[longest] + 1) % drawn.shape[longest]] + spot[longest + 1:]
    return drawn.at[tuple(spot)].set(smallest).at[tuple(neighbour)].set(top_value)


def shard_levels(stream_key, dims, cuts, low, top_value):
    factor_of = 1.0
    for dim, shards_of in cuts:
        steps = jax.random.uniform(jax.random.fold_in(jax.random.fold_in(stream_key, 6), dim), (shards_of,), jnp.float32, low / len(cuts), top_value / len(cuts))
        factor_of = factor_of * jnp.repeat(jnp.exp(steps), dims[dim] // shards_of).reshape((-1,) + (1,) * (len(dims) - 1 - dim))
    return factor_of


def centred(own_key, extent, spread, most, pieces=(), held_as=jnp.bfloat16):
    gain = shard_levels(own_key, extent, pieces, -0.22, 0.18) if pieces else 1.0
    entries = jax.random.normal(own_key, extent, jnp.float32) * spread * gain
    return jnp.minimum(jnp.maximum(entries, -most), most).astype(held_as)


def setup_inputs(seed: int = 0) -> dict:
    splits = jax.random.split(jax.random.key(seed), 6)
    queries = draw_queries(jax.random.fold_in(splits[5], 71), 0)
    positives = centred(splits[1], (GROUPS, Q_COL, S, D), 1.0, 6.0, ((0, 32), (1, 16)))
    memory = centred(splits[2], (GROUPS, P_COL, S, D), 1.0, 6.0, ((0, 32), (1, 16)))
    candidates = draw_candidates(jax.random.fold_in(splits[5], 71), 0)
    counts = place_ends(jax.random.randint(splits[4], (GROUPS, Q_COL), C // 4, C // 2 + 1), jax.random.fold_in(splits[4], 1), C // 4, (C // 2 + 1) - 1).astype(jnp.int32)
    return dict(queries=queries, positives=positives, memory=memory, candidates=candidates, counts=counts)


def maxsim(query_tokens, passages):
    product = jnp.einsum("qd,nsd->nqs", query_tokens.astype(jnp.float32), passages.astype(jnp.float32))
    return jnp.sum(jnp.max(product, axis=2), axis=1)


def reference(queries, positives, memory, candidates, counts):
    flat_queries = queries.reshape(GROUPS * Q_COL, QT, D)
    flat_candidates = candidates.reshape(GROUPS * Q_COL, C)
    flat_counts = counts.reshape(GROUPS * Q_COL)
    slot_iota = jnp.arange(C, dtype=jnp.int32)
    batch_iota = jnp.arange(N_GROUP * Q_DEV, dtype=jnp.int32)

    def one_query(flat_index):
        group_index = flat_index // Q_COL
        inner = flat_index % Q_COL
        block = inner // Q_DEV
        query_tokens = flat_queries[flat_index]
        block_pos = lax.dynamic_slice_in_dim(positives, (block * Q_DEV).astype(jnp.int32), Q_DEV, 1)
        block_pos = block_pos.reshape(N_GROUP * Q_DEV, S, D)
        batch_row = maxsim(query_tokens, block_pos)
        column = memory[group_index]
        chosen = column[flat_candidates[flat_index]]
        valid = slot_iota < flat_counts[flat_index]
        raw = maxsim(query_tokens, chosen)
        memory_row = jnp.where(valid, raw, jnp.float32(0.0))
        top = jnp.maximum(jnp.max(batch_row), jnp.max(jnp.where(valid, raw, -jnp.inf)))
        total = jnp.sum(jnp.exp(batch_row - top)) + jnp.sum(jnp.where(valid, jnp.exp(raw - top), jnp.float32(0.0)))
        own_index = group_index * Q_DEV + inner % Q_DEV
        target = jnp.sum(jnp.where(batch_iota == own_index, batch_row, jnp.float32(0.0)))
        return batch_row, memory_row, top + jnp.log(total) - target

    batch_rows, memory_rows, losses = lax.map(one_query, jnp.arange(GROUPS * Q_COL, dtype=jnp.int32))
    return (batch_rows.reshape(GROUPS, Q_COL, N_GROUP * Q_DEV), memory_rows.reshape(GROUPS, Q_COL, C), losses.reshape(GROUPS, Q_COL))
```

```python
import functools
import math

import jax
import jax.numpy as jnp
from jax import lax
from jax.experimental import pallas as pl
from jax.experimental.pallas import tpu as pltpu
from jax.sharding import PartitionSpec as P

MESH = pl.DeviceIdType.MESH
F32 = jnp.float32
BF16 = jnp.bfloat16
I32 = jnp.int32
CAP = 24
Q = 8
TOK = 32
LIVE = 32
LANES = 128
COLS = Q * TOK


def iota(shape, axis):
    return lax.broadcasted_iota(I32, shape, axis)


def kernel(zs, side, q_hbm, pos_hbm, mem_hbm, cand_ref, cnt_ref, out_b, out_m, out_l,
           qv, posv, memv, zbuf, gbuf, ask_out, ask_in, ids, row_out, row_in, tile_out, tile_in,
           load_sem, zr_sem, zl_sem, cls_sem, sib_sem, ask_sem, row_sem, tile_sem,
           zsend_sem, gsend_sem, ask_send_sem, row_send_sem, tile_send_sem):
    half = zs // 2
    plane = side * side
    ng = 2 * plane
    items = zs - 1
    feat = LANES // 2

    z = lax.axis_index("memory")
    g = lax.axis_index("group")
    core = lax.rem(g, 2)
    px = lax.rem(g // 2, side)
    py = g // (2 * side)
    z_right = lax.rem(z + 1, zs)
    z_left = lax.rem(z + zs - 1, zs)
    sibling = g + 1 - 2 * core

    def source(k, c):
        a = lax.rem(k, side)
        b = k // side
        dx = a + c * (b - a)
        dy = b + c * (a - b)
        return (lax.rem(py - dy + side, side) * side + lax.rem(px - dx + side, side)) * 2 + c

    def target(a, b):
        dx = a + core * (b - a)
        dy = b + core * (a - b)
        return (lax.rem(py + dy, side) * side + lax.rem(px + dx, side)) * 2 + core

    load_q = pltpu.make_async_copy(q_hbm, qv, load_sem.at[0])
    load_q.start()
    load_pos = pltpu.make_async_copy(pos_hbm, posv, load_sem.at[1])
    load_mem = pltpu.make_async_copy(mem_hbm, memv, load_sem.at[2])
    load_pos.start()
    load_mem.start()

    barrier = pltpu.get_barrier_semaphore()

    def greet_z(i, _):
        pl.semaphore_signal(barrier, inc=1, device_id=(lax.rem(z + i, zs), g), device_id_type=MESH)
        return 0

    def greet_g(i, _):
        pl.semaphore_signal(barrier, inc=1, device_id=(z, lax.rem(g + i, ng)), device_id_type=MESH)
        return 0

    lax.fori_loop(1, zs, greet_z, 0)
    lax.fori_loop(1, ng, greet_g, 0)

    lane = iota((1, LANES), 1)
    cand = jnp.concatenate([cand_ref[...], jnp.zeros((Q, LANES - cand_ref.shape[1]), I32)], axis=1)
    parts, limits = [], []
    for h in range(2):
        flat = jnp.zeros((1, LANES), I32)
        limit = jnp.zeros((1, LANES), I32)
        for j in range(4):
            row = cand[4 * h + j : 4 * h + j + 1]
            if j:
                row = pltpu.roll(row, j * LIVE, 1)
            flat = jnp.where(lane // LIVE == j, row, flat)
            limit = jnp.where(lane // LIVE == j, cnt_ref[0, 4 * h + j], limit)
        parts.append(flat)
        limits.append(limit)
    flat = jnp.concatenate(parts, axis=1)
    limit = jnp.concatenate(limits, axis=1)
    slot = iota((1, COLS), 1)
    live = (slot % LIVE) < limit
    holds = LANES
    owner = jnp.where(live, flat // holds, -1)
    local = (flat % holds).astype(F32)
    query = (slot // LIVE).astype(F32)
    onehot = jnp.where(iota((zs, COLS), 0) == owner, 1.0, 0.0).astype(F32)
    upper = jnp.where(iota((COLS, COLS), 0) < iota((COLS, COLS), 1), 1.0, 0.0).astype(BF16)
    before = jnp.dot(onehot.astype(BF16), upper, preferred_element_type=F32)
    rank = jnp.sum(onehot * before, axis=0, keepdims=True)
    place = (iota((LANES, COLS), 0).astype(F32) == rank)
    both = jnp.concatenate([onehot * local, onehot * query], axis=0).astype(BF16)
    table = lax.dot_general(
        both, jnp.where(place, 1.0, 0.0).astype(BF16), (((1,), (1,)), ((), ())), preferred_element_type=F32
    )
    code = (table[:zs] + 128.0 * table[zs:]).astype(I32)
    for o in range(zs):
        ask_out[o] = code[o : o + 1]

    load_q.wait()
    turned = qv[...].astype(F32).T.astype(BF16)
    zbuf[z] = turned
    gbuf[g] = turned
    ask_in[z] = ask_out[z]

    pl.semaphore_wait(barrier, zs - 1 + ng - 1)

    def piece(i):
        return i // 2 + 1, lax.rem(i, 2) * feat

    def z_copy(block, first, sem, to):
        ref = zbuf.at[block, pl.ds(pl.multiple_of(first, feat), feat)]
        return pltpu.make_async_remote_copy(
            src_ref=ref, dst_ref=ref, send_sem=zsend_sem, recv_sem=sem,
            device_id=(to, g), device_id_type=MESH,
        )

    def right_send(i):
        d, first = piece(i)
        return z_copy(lax.rem(z - d + 1 + zs, zs), first, zr_sem.at[i], z_right)

    def left_send(i):
        d, first = piece(i)
        first = jnp.where(i == items - 1, feat, first)
        return z_copy(lax.rem(z + d - 1, zs), first, zl_sem.at[i], z_left)

    def right_wait(i):
        d, first = piece(i)
        z_copy(lax.rem(z - d + zs, zs), first, zr_sem.at[i], z_right).wait_recv()

    def left_wait(i):
        d, first = piece(i)
        first = jnp.where(i == items - 1, feat, first)
        z_copy(lax.rem(z + d, zs), first, zl_sem.at[i], z_left).wait_recv()

    def g_copy(block, sem, to):
        ref = gbuf.at[block]
        return pltpu.make_async_remote_copy(
            src_ref=ref, dst_ref=ref, send_sem=gsend_sem, recv_sem=sem,
            device_id=(z, to), device_id_type=MESH,
        )

    for i in range(min(2, items)):
        right_send(jnp.int32(i)).start()
        left_send(jnp.int32(i)).start()
    for a in range(1, side):
        g_copy(g, cls_sem.at[a], target(a, 0)).start()
    g_copy(g, sib_sem.at[0], sibling).start()
    for b in range(1, side):
        g_copy(g, cls_sem.at[b * side], target(0, b)).start()

    def ask(i, _):
        to = lax.rem(z + i, zs)
        pltpu.make_async_remote_copy(
            src_ref=ask_out.at[to], dst_ref=ask_in.at[z], send_sem=ask_send_sem, recv_sem=ask_sem,
            device_id=(to, g), device_id_type=MESH,
        ).start()
        return 0

    lax.fori_loop(1, zs, ask, 0)

    def best(passages, tokens):
        r = jnp.dot(passages, tokens, preferred_element_type=F32)
        return jnp.max(r.reshape(passages.shape[0] // LANES, LANES, COLS), axis=1)

    lane8 = iota((8, LANES), 1)

    def batch(block):
        m = best(posv[...], gbuf[block])
        x0, x1 = m[:, :LANES], m[:, LANES:]
        x0 = x0 + pltpu.roll(x0, LANES - 16, 1)
        x1 = x1 + pltpu.roll(x1, LANES - 16, 1)
        x = jnp.where(lane8 % 32 < 16, x0, pltpu.roll(x1, 16, 1))
        for s in (8, 4, 2, 1):
            x = x + pltpu.roll(x, LANES - s, 1)
        return x

    def batch_send(block):
        tile_out[block] = batch(block)
        pltpu.make_async_remote_copy(
            src_ref=tile_out.at[block], dst_ref=tile_in.at[g], send_sem=tile_send_sem, recv_sem=tile_sem,
            device_id=(z, block), device_id_type=MESH,
        ).start()

    diag = iota((CAP, LANES), 0) == iota((CAP, LANES), 1)
    col_query = iota((CAP, COLS), 1) // TOK

    def memory_rows(asker):
        tokens = zbuf[asker]
        rows = []
        for first in range(0, CAP, 8):
            passages = jnp.concatenate([memv[ids[asker, 0, first + j] & (holds - 1)] for j in range(8)], axis=0)
            rows.append(best(passages, tokens))
        m = jnp.concatenate(rows, axis=0)
        asked = jnp.sum(jnp.where(diag, ask_in[asker].astype(F32), 0.0), axis=1, keepdims=True)
        asked = asked.astype(I32) // holds
        s = jnp.sum(jnp.where(col_query == asked, m, 0.0), axis=1, keepdims=True)
        return jnp.sum(jnp.where(diag, s, 0.0), axis=0, keepdims=True)

    def memory_send(asker):
        row_out[asker] = memory_rows(asker)
        pltpu.make_async_remote_copy(
            src_ref=row_out.at[asker], dst_ref=row_in.at[z], send_sem=row_send_sem, recv_sem=row_sem,
            device_id=(asker, g), device_id_type=MESH,
        ).start()

    load_pos.wait()
    tile_in[g] = batch(g)

    for a in range(1, side):
        k = jnp.int32(a)
        block = source(k, core)
        g_copy(block, cls_sem.at[a], sibling).wait_recv()
        g_copy(block, sib_sem.at[a], sibling).start()
        for b in range(1, side):
            g_copy(block, cls_sem.at[b * side + a], target(0, b)).start()

    pltpu.make_async_copy(ask_in.at[pl.ds(0, zs - 1)], ask_in.at[pl.ds(0, zs - 1)], ask_sem).wait()
    load_ids = pltpu.make_async_copy(ask_in, ids, load_sem.at[3])
    load_ids.start()
    load_ids.wait()
    load_mem.wait()
    row_in[z] = memory_rows(z)

    def step(t, _):
        right_wait(t)

        @pl.when(t + 2 <= items - 1)
        def _():
            right_send(t + 2).start()

        left_wait(t)

        @pl.when(t + 2 <= items - 2)
        def _():
            left_send(t + 2).start()

        @pl.when(t == items - 2)
        def _():
            left_send(t + 1).start()

        k = t + 1
        block = source(k, core)

        @pl.when(k >= side)
        def _():
            g_copy(block, cls_sem.at[k], sibling).wait_recv()
            g_copy(block, sib_sem.at[k], sibling).start()

        other = source(t, 1 - core)
        g_copy(other, sib_sem.at[t], sibling).wait_recv()

        @pl.when(t > 0)
        def _():
            d = (t + 1) // 2
            odd = lax.rem(t, 2)
            memory_send(jnp.where(odd == 1, lax.rem(z - d + zs, zs), lax.rem(z + d, zs)))

        batch_send(block)
        batch_send(other)
        return 0

    lax.fori_loop(0, items, step, 0)

    memory_send(lax.rem(z + half, zs))
    last = source(jnp.int32(items), 1 - core)
    g_copy(last, sib_sem.at[items], sibling).wait_recv()
    batch_send(last)

    pltpu.make_async_copy(row_in.at[pl.ds(0, zs - 1)], row_in.at[pl.ds(0, zs - 1)], row_sem).wait()
    got = jnp.concatenate([row_in[o] for o in range(zs)], axis=0)
    spread = lax.dot_general(
        got, onehot, (((0,), (0,)), ((), ())), preferred_element_type=F32, precision=lax.Precision.HIGHEST
    )
    picked = jnp.sum(jnp.where(place, spread, 0.0), axis=0, keepdims=True)
    sub8 = iota((Q, LANES), 0)
    scores = jnp.zeros((Q, LANES), F32)
    count = jnp.zeros((Q, LANES), I32)
    for q in range(Q):
        h, j = q // 4, q % 4
        row = picked[:, h * LANES : (h + 1) * LANES]
        if j:
            row = pltpu.roll(row, LANES - j * LIVE, 1)
        scores = jnp.where(sub8 == q, row, scores)
        count = jnp.where(sub8 == q, cnt_ref[0, q], count)
    valid = lane8 < count
    scores = jnp.where(valid, scores, 0.0)
    out_m[...] = scores[:, : out_m.shape[1]]

    pltpu.make_async_copy(tile_in.at[pl.ds(0, ng - 1)], tile_in.at[pl.ds(0, ng - 1)], tile_sem).wait()
    turned_scores = tile_in[...].reshape(ng * 8, LANES).T
    order = [0, 32, 64, 96, 16, 48, 80, 112]
    rows = jnp.concatenate([turned_scores[o : o + 1] for o in order], axis=0)
    out_b[...] = rows
    top = jnp.maximum(
        jnp.max(rows, axis=1, keepdims=True),
        jnp.max(jnp.where(valid, scores, -jnp.inf), axis=1, keepdims=True),
    )
    total = jnp.sum(jnp.exp(rows - top), axis=1, keepdims=True) + jnp.sum(
        jnp.where(valid, jnp.exp(scores - top), 0.0), axis=1, keepdims=True
    )
    mine = iota(rows.shape, 1) == g * Q + iota(rows.shape, 0)
    own = jnp.sum(jnp.where(mine, rows, 0.0), axis=1, keepdims=True)
    loss = top + jnp.log(total) - own
    spread_loss = jnp.where(lane8 == sub8, loss, 0.0)
    out_l[...] = jnp.sum(spread_loss, axis=0, keepdims=True)[:, :Q]

    pltpu.make_async_copy(zbuf.at[pl.ds(0, items)], zbuf.at[pl.ds(0, items)], zsend_sem).wait()
    pltpu.make_async_copy(gbuf.at[pl.ds(0, ng - 1)], gbuf.at[pl.ds(0, ng - 1)], gsend_sem).wait()
    pltpu.make_async_copy(ask_in.at[pl.ds(0, items)], ask_in.at[pl.ds(0, items)], ask_send_sem).wait()
    pltpu.make_async_copy(row_in.at[pl.ds(0, items)], row_in.at[pl.ds(0, items)], row_send_sem).wait()
    pltpu.make_async_copy(tile_in.at[pl.ds(0, ng - 1)], tile_in.at[pl.ds(0, ng - 1)], tile_send_sem).wait()


def body(queries, positives, memory, candidates, counts):
    zs = lax.axis_size("memory")
    ng = lax.axis_size("group")
    side = math.isqrt(ng // 2)
    assert ng == 2 * side * side and zs == side * side
    width = queries.shape[3]
    p_local = memory.shape[1]
    any_space = pl.BlockSpec(memory_space=pl.ANY)
    vmem = pl.BlockSpec(memory_space=pltpu.VMEM)
    smem = pl.BlockSpec(memory_space=pltpu.SMEM)
    dma = pltpu.SemaphoreType.DMA
    slots = candidates.shape[2]
    out_b, out_m, out_l = pl.pallas_call(
        functools.partial(kernel, zs, side),
        out_shape=(
            jax.ShapeDtypeStruct((Q, ng * Q), F32),
            jax.ShapeDtypeStruct((Q, slots), F32),
            jax.ShapeDtypeStruct((1, Q), F32),
        ),
        in_specs=[any_space, any_space, any_space, vmem, smem],
        out_specs=(vmem, vmem, vmem),
        scratch_shapes=[
            pltpu.VMEM((COLS, width), BF16),
            pltpu.VMEM((Q * LANES, width), BF16),
            pltpu.VMEM((p_local, LANES, width), BF16),
            pltpu.VMEM((zs, width, COLS), BF16),
            pltpu.VMEM((ng, width, COLS), BF16),
            pltpu.VMEM((zs, 1, LANES), I32),
            pltpu.VMEM((zs, 1, LANES), I32),
            pltpu.SMEM((zs, 1, LANES), I32),
            pltpu.VMEM((zs, 1, LANES), F32),
            pltpu.VMEM((zs, 1, LANES), F32),
            pltpu.VMEM((ng, 8, LANES), F32),
            pltpu.VMEM((ng, 8, LANES), F32),
            dma((4,)), dma((zs - 1,)), dma((zs - 1,)), dma((ng // 2,)), dma((ng // 2,)),
            dma, dma, dma,
            dma, dma, dma, dma, dma,
        ],
        compiler_params=pltpu.CompilerParams(
            collective_id=0, has_side_effects=True, vmem_limit_bytes=40 * 1024 * 1024
        ),
        cost_estimate=pl.CostEstimate(flops=5 * 10**9, bytes_accessed=5 * 10**6, transcendentals=4096),
        name="scores",
    )(
        queries[0].reshape(COLS, width),
        positives[0].reshape(Q * LANES, width),
        memory[0],
        candidates[0],
        counts,
    )
    return out_b[None], out_m[None], out_l


def solution(mesh):
    in_specs = (
        P("group", "memory", None, None),
        P("group", "memory", None, None),
        P("group", "memory", None, None),
        P("group", "memory", None),
        P("group", "memory"),
    )
    out_specs = (P("group", "memory", None), P("group", "memory", None), P("group", "memory"))
    return jax.shard_map(body, mesh=mesh, in_specs=in_specs, out_specs=out_specs, check_vma=False)
```

```python
import functools
import math

import jax
import jax.numpy as jnp
from jax import lax
from jax.experimental import pallas as pl
from jax.experimental.pallas import tpu as pltpu
from jax.sharding import PartitionSpec as P

MESH = pl.DeviceIdType.MESH
F32 = jnp.float32
BF16 = jnp.bfloat16
I32 = jnp.int32
CAP = 24
Q = 8
TOK = 32
LIVE = 32
LANES = 128
COLS = Q * TOK
CHUNKS = 4


def iota(shape, axis):
    return lax.broadcasted_iota(I32, shape, axis)


def kernel(zs, side, q_hbm, pos_hbm, mem_hbm, cand_ref, cnt_ref, out_b, out_m, out_l,
           qv, posv, memv, zbuf, gbuf, asks, ids, best_b, best_m, row_out, row_in, tile_out, tile_in,
           load_sem, zr_sem, zl_sem, ar_sem, al_sem, id_sem, cls_sem, sib_sem, row_sem, tile_sem,
           zsend_sem, asend_sem, gsend_sem, row_send_sem, tile_send_sem):
    half = zs // 2
    plane = side * side
    ng = 2 * plane
    side_bits = side.bit_length() - 1
    rows_of = LANES // CHUNKS

    z = lax.axis_index("memory")
    g = lax.axis_index("group")
    core = g & 1
    px = (g >> 1) & (side - 1)
    py = g >> (1 + side_bits)
    z_right = (z + 1) & (zs - 1)
    z_left = (z + zs - 1) & (zs - 1)
    sibling = g + 1 - 2 * core

    def source(k, c):
        a, b = k % side, k // side
        dx = a + c * (b - a)
        dy = b + c * (a - b)
        return (((py - dy) & (side - 1)) * side + ((px - dx) & (side - 1))) * 2 + c

    def target(a, b):
        dx = a + core * (b - a)
        dy = b + core * (a - b)
        return (((py + dy) & (side - 1)) * side + ((px + dx) & (side - 1))) * 2 + core

    def block_of(n):
        return source(n, core) if n < plane else source(n - plane, 1 - core)

    load_q = pltpu.make_async_copy(q_hbm, qv, load_sem.at[0])
    load_pos = pltpu.make_async_copy(pos_hbm, posv, load_sem.at[1])
    load_mem = pltpu.make_async_copy(mem_hbm, memv, load_sem.at[2])
    load_q.start()
    load_pos.start()
    load_mem.start()

    barrier = pltpu.get_barrier_semaphore()
    partners = [(z_right, g), (z_left, g), (z, sibling)]
    for a in range(1, side):
        partners += [(z, target(a, 0)), (z, target(0, a))]
    for to in partners:
        pl.semaphore_signal(barrier, inc=1, device_id=to, device_id_type=MESH)

    lane = iota((1, LANES), 1)
    cand = jnp.concatenate([cand_ref[...], jnp.zeros((Q, LANES - cand_ref.shape[1]), I32)], axis=1)
    parts, limits = [], []
    for h in range(2):
        flat = jnp.zeros((1, LANES), I32)
        limit = jnp.zeros((1, LANES), I32)
        for j in range(4):
            row = cand[4 * h + j : 4 * h + j + 1]
            if j:
                row = pltpu.roll(row, j * LIVE, 1)
            flat = jnp.where(lane >> 5 == j, row, flat)
            limit = jnp.where(lane >> 5 == j, cnt_ref[0, 4 * h + j], limit)
        parts.append(flat)
        limits.append(limit)
    flat = jnp.concatenate(parts, axis=1)
    limit = jnp.concatenate(limits, axis=1)
    slot = iota((1, COLS), 1)
    live = (slot & (LIVE - 1)) < limit
    owner = jnp.where(live, flat >> 7, -1)
    local = (flat & (LANES - 1)).astype(F32)
    query = (slot >> 5).astype(F32)
    onehot = jnp.where(iota((zs, COLS), 0) == owner, 1.0, 0.0).astype(F32)
    upper = jnp.where(iota((COLS, COLS), 0) < iota((COLS, COLS), 1), 1.0, 0.0).astype(BF16)
    before = jnp.dot(onehot.astype(BF16), upper, preferred_element_type=F32)
    rank = jnp.sum(onehot * before, axis=0, keepdims=True)
    place = iota((LANES, COLS), 0).astype(F32) == rank
    both = jnp.concatenate([onehot * local, onehot * query], axis=0).astype(BF16)
    table = lax.dot_general(
        both, jnp.where(place, 1.0, 0.0).astype(BF16), (((1,), (1,)), ((), ())), preferred_element_type=F32
    )
    code = (table[:zs] + 128.0 * table[zs:]).astype(I32)
    for o in range(zs // 2):
        asks[z, o] = code[2 * o : 2 * o + 1] + pltpu.roll(code[2 * o + 1 : 2 * o + 2], 64, 1)

    load_q.wait()
    turned = qv[...].astype(F32).T.astype(BF16)
    zbuf[z] = turned
    gbuf[g] = turned

    pl.semaphore_wait(barrier, len(partners))

    def ring_copy(ref, send, recv, to):
        return pltpu.make_async_remote_copy(
            src_ref=ref, dst_ref=ref, send_sem=send, recv_sem=recv, device_id=(to, g), device_id_type=MESH
        )

    def right(d, c, step):
        block = (z - d + step) & (zs - 1)
        ref = zbuf.at[block, pl.ds(c * rows_of, rows_of)]
        return ring_copy(ref, zsend_sem, zr_sem.at[(d - 1) * CHUNKS + c], z_right)

    def left(d, c, step):
        block = (z + d - step) & (zs - 1)
        ref = zbuf.at[block, pl.ds(c * rows_of, rows_of)]
        return ring_copy(ref, zsend_sem, zl_sem.at[(d - 1) * CHUNKS + c], z_left)

    def right_ask(d, step):
        return ring_copy(asks.at[(z - d + step) & (zs - 1)], asend_sem, ar_sem.at[d - 1], z_right)

    def left_ask(d, step):
        return ring_copy(asks.at[(z + d - step) & (zs - 1)], asend_sem, al_sem.at[d - 1], z_left)

    def by_right(d, c):
        return d < half or (d == half and c < CHUNKS // 2)

    def by_left(d, c):
        return d < half or (d == half and c >= CHUNKS // 2)

    def g_copy(block, sem, to):
        ref = gbuf.at[block]
        return pltpu.make_async_remote_copy(
            src_ref=ref, dst_ref=ref, send_sem=gsend_sem, recv_sem=sem,
            device_id=(z, to), device_id_type=MESH,
        )

    def asker_of(n):
        d = (n + 1) // 2
        return (z - d if n % 2 else z + d) & (zs - 1)

    def load_ids(n):
        return pltpu.make_async_copy(asks.at[asker_of(n), z >> 1], ids.at[n], id_sem.at[n])

    right_ask(1, 1).start()
    if half > 1:
        left_ask(1, 1).start()
    for c in range(CHUNKS):
        if by_right(1, c):
            right(1, c, 1).start()
        if by_left(1, c):
            left(1, c, 1).start()
    for a in range(1, side):
        g_copy(g, cls_sem.at[a], target(a, 0)).start()
    g_copy(g, sib_sem.at[0], sibling).start()
    for b in range(1, side):
        g_copy(g, cls_sem.at[b * side], target(0, b)).start()
    load_ids(0).start()

    def best(passages, tokens):
        r = jnp.dot(passages, tokens, preferred_element_type=F32)
        return jnp.max(r.reshape(passages.shape[0] // LANES, LANES, COLS), axis=1)

    lane8 = iota((8, LANES), 1)

    def batch_unit(n):
        best_b[n] = best(posv[...], gbuf[block_of(n)])

    def batch_finish(ns):
        for n in ns:
            x0, x1 = best_b[n, :, :LANES], best_b[n, :, LANES:]
            x0 = x0 + pltpu.roll(x0, LANES - 16, 1)
            x1 = x1 + pltpu.roll(x1, LANES - 16, 1)
            x = jnp.where((lane8 & 31) < 16, x0, pltpu.roll(x1, 16, 1))
            for s in (8, 4, 2, 1):
                x = x + pltpu.roll(x, LANES - s, 1)
            if n == 0:
                tile_in[g] = x
            else:
                tile_out[n] = x

    def batch_send(ns):
        for n in ns:
            if n:
                pltpu.make_async_remote_copy(
                    src_ref=tile_out.at[n], dst_ref=tile_in.at[g], send_sem=tile_send_sem, recv_sem=tile_sem,
                    device_id=(z, block_of(n)), device_id_type=MESH,
                ).start()

    diag = iota((CAP, LANES), 0) == iota((CAP, LANES), 1)
    col_query = iota((CAP, COLS), 1) >> 5
    upper_half = (z & 1) * 64

    def memory_unit(n, part):
        first = part * 8
        passages = jnp.concatenate(
            [memv[ids[n, 0, upper_half + first + j] & (LANES - 1)] for j in range(8)], axis=0
        )
        best_m[n, pl.ds(first, 8)] = best(passages, zbuf[asker_of(n)])

    def memory_finish(ns):
        for n in ns:
            row = asks[asker_of(n), z >> 1].astype(F32)
            row = jnp.where(upper_half > 0, pltpu.roll(row, 64, 1), row)
            asked = jnp.sum(jnp.where(diag, row, 0.0), axis=1, keepdims=True).astype(I32) >> 7
            s = jnp.sum(jnp.where(col_query == asked, best_m[n], 0.0), axis=1, keepdims=True)
            scores = jnp.sum(jnp.where(diag, s, 0.0), axis=0, keepdims=True)
            if n == 0:
                row_in[z] = scores
            else:
                row_out[n] = scores

    def memory_send(ns):
        for n in ns:
            if n:
                pltpu.make_async_remote_copy(
                    src_ref=row_out.at[n], dst_ref=row_in.at[z], send_sem=row_send_sem, recv_sem=row_sem,
                    device_id=(asker_of(n), g), device_id_type=MESH,
                ).start()

    turns = CHUNKS * (half - 1) + CHUNKS // 2
    moves = [[] for _ in range(turns + 4)]
    sums = [[] for _ in range(turns + 4)]

    def z_turn(d, c):
        def ask():
            right_ask(d, 0).wait_recv()
            if d < half:
                right_ask(d + 1, 1).start()
                left_ask(d, 0).wait_recv()
                if d + 1 < half:
                    left_ask(d + 1, 1).start()
                load_ids(2 * d).start()
            load_ids(2 * d - 1).start()

        def run():
            if c == 0:
                ask()
            if d < half:
                right(d, c, 0).wait_recv()
                if by_right(d + 1, c):
                    right(d + 1, c, 1).start()
                left(d, c, 0).wait_recv()
                if by_left(d + 1, c):
                    left(d + 1, c, 1).start()
            else:
                right(d, c, 0).wait_recv()
                left(d, c + CHUNKS // 2, 0).wait_recv()

        return run

    for t in range(turns):
        moves[t].append(z_turn(t // CHUNKS + 1, t % CHUNKS))

    def cls_arrives(k):
        def run():
            block = source(k, core)
            g_copy(block, cls_sem.at[k], sibling).wait_recv()
            if k < side:
                for b in range(1, side):
                    g_copy(block, cls_sem.at[b * side + k], target(0, b)).start()
            g_copy(block, sib_sem.at[k], sibling).start()

        return run

    def sib_arrives(k):
        return lambda: g_copy(source(k, 1 - core), sib_sem.at[k], sibling).wait_recv()

    order = [(0, 0)]
    for k in range(1, plane):
        t = 0 if k < side else min(turns - 1, side + 5 * (k - side) // 4)
        moves[t].append(cls_arrives(k))
        order.append((max(t, min(turns - 1, 2 * k - 2)), k))
    for k in range(plane):
        t = min(turns, 2 * k + 1)
        moves[t].append(sib_arrives(k))
        order.append((t, plane + k))
    order.sort()
    first = 0
    while first < ng:
        ns = [n for _, n in order[first : first + 8]]
        last_turn = order[min(ng, first + 8) - 1][0]
        sums[last_turn + 1].append(functools.partial(batch_finish, ns))
        moves[last_turn + 2].append(functools.partial(batch_send, ns))
        first += 8
    for t, n in order:
        sums[t].append(functools.partial(batch_unit, n))

    def ids_arrive(ns):
        for n in ns:
            load_ids(n).wait()

    def mem_start():
        load_mem.wait()
        load_pos.wait()
        ids_arrive([0])

    moves[0].insert(0, mem_start)
    for part in range(3):
        sums[0].append(functools.partial(memory_unit, 0, part))
    sums[1].append(functools.partial(memory_finish, [0]))
    for d in range(1, half + 1):
        ns = [2 * d - 1, 2 * d] if d < half else [2 * d - 1]
        start = CHUNKS * d - 1 if d < half else turns - 1
        moves[start].append(functools.partial(ids_arrive, ns))
        units = [(n, part) for n in ns for part in range(3)]
        spread = CHUNKS if d + 1 < half else 2
        if d == half:
            spread = 1
        for i, (n, part) in enumerate(units):
            sums[start + i * spread // len(units)].append(functools.partial(memory_unit, n, part))
        sums[start + spread].append(functools.partial(memory_finish, ns))
        moves[start + spread + 1].append(functools.partial(memory_send, ns))

    for t in range(turns + 4):
        for move in moves[t]:
            move()
        for work in sums[t]:
            work()

    pltpu.make_async_copy(row_in.at[pl.ds(0, zs - 1)], row_in.at[pl.ds(0, zs - 1)], row_sem).wait()
    got = jnp.concatenate([row_in[o] for o in range(zs)], axis=0)
    spread = lax.dot_general(
        got, onehot, (((0,), (0,)), ((), ())), preferred_element_type=F32, precision=lax.Precision.HIGHEST
    )
    picked = jnp.sum(jnp.where(place, spread, 0.0), axis=0, keepdims=True)
    sub8 = iota((Q, LANES), 0)
    scores = jnp.zeros((Q, LANES), F32)
    count = jnp.zeros((Q, LANES), I32)
    for q in range(Q):
        h, j = q // 4, q % 4
        row = picked[:, h * LANES : (h + 1) * LANES]
        if j:
            row = pltpu.roll(row, LANES - j * LIVE, 1)
        scores = jnp.where(sub8 == q, row, scores)
        count = jnp.where(sub8 == q, cnt_ref[0, q], count)
    valid = lane8 < count
    scores = jnp.where(valid, scores, 0.0)
    out_m[...] = scores[:, : out_m.shape[1]]

    pltpu.make_async_copy(tile_in.at[pl.ds(0, ng - 1)], tile_in.at[pl.ds(0, ng - 1)], tile_sem).wait()
    turned_scores = tile_in[...].reshape(ng * 8, LANES).T
    order = [0, 32, 64, 96, 16, 48, 80, 112]
    rows = jnp.concatenate([turned_scores[o : o + 1] for o in order], axis=0)
    out_b[...] = rows
    top = jnp.maximum(
        jnp.max(rows, axis=1, keepdims=True),
        jnp.max(jnp.where(valid, scores, -jnp.inf), axis=1, keepdims=True),
    )
    total = jnp.sum(jnp.exp(rows - top), axis=1, keepdims=True) + jnp.sum(
        jnp.where(valid, jnp.exp(scores - top), 0.0), axis=1, keepdims=True
    )
    mine = iota(rows.shape, 1) == g * Q + iota(rows.shape, 0)
    own = jnp.sum(jnp.where(mine, rows, 0.0), axis=1, keepdims=True)
    loss = top + jnp.log(total) - own
    spread_loss = jnp.where(lane8 == sub8, loss, 0.0)
    out_l[...] = jnp.sum(spread_loss, axis=0, keepdims=True)[:, :Q]

    items = zs - 1
    pltpu.make_async_copy(zbuf.at[pl.ds(0, items)], zbuf.at[pl.ds(0, items)], zsend_sem).wait()
    pltpu.make_async_copy(gbuf.at[pl.ds(0, ng - 1)], gbuf.at[pl.ds(0, ng - 1)], gsend_sem).wait()
    pltpu.make_async_copy(asks.at[pl.ds(0, items)], asks.at[pl.ds(0, items)], asend_sem).wait()
    pltpu.make_async_copy(row_in.at[pl.ds(0, items)], row_in.at[pl.ds(0, items)], row_send_sem).wait()
    pltpu.make_async_copy(tile_in.at[pl.ds(0, ng - 1)], tile_in.at[pl.ds(0, ng - 1)], tile_send_sem).wait()


def body(queries, positives, memory, candidates, counts):
    zs = lax.axis_size("memory")
    ng = lax.axis_size("group")
    side = math.isqrt(ng // 2)
    assert ng == 2 * side * side and zs == side * side
    width = queries.shape[3]
    p_local = memory.shape[1]
    any_space = pl.BlockSpec(memory_space=pltpu.HBM)
    vmem = pl.BlockSpec(memory_space=pltpu.VMEM)
    smem = pl.BlockSpec(memory_space=pltpu.SMEM)
    dma = pltpu.SemaphoreType.DMA
    slots = candidates.shape[2]
    out_b, out_m, out_l = pl.pallas_call(
        functools.partial(kernel, zs, side),
        out_shape=(
            jax.ShapeDtypeStruct((Q, ng * Q), F32),
            jax.ShapeDtypeStruct((Q, slots), F32),
            jax.ShapeDtypeStruct((1, Q), F32),
        ),
        in_specs=[any_space, any_space, any_space, vmem, smem],
        out_specs=(vmem, vmem, vmem),
        scratch_shapes=[
            pltpu.VMEM((COLS, width), BF16),
            pltpu.VMEM((Q * LANES, width), BF16),
            pltpu.VMEM((p_local, LANES, width), BF16),
            pltpu.VMEM((zs, width, COLS), BF16),
            pltpu.VMEM((ng, width, COLS), BF16),
            pltpu.VMEM((zs, zs // 2, 1, LANES), I32),
            pltpu.SMEM((zs, 1, LANES), I32),
            pltpu.VMEM((ng, 8, COLS), F32),
            pltpu.VMEM((zs, CAP, COLS), F32),
            pltpu.VMEM((zs, 1, LANES), F32),
            pltpu.VMEM((zs, 1, LANES), F32),
            pltpu.VMEM((ng, 8, LANES), F32),
            pltpu.VMEM((ng, 8, LANES), F32),
            dma((3,)), dma((zs // 2 * CHUNKS,)), dma((zs // 2 * CHUNKS,)), dma((zs // 2,)), dma((zs // 2,)),
            dma((zs,)), dma((ng // 2,)), dma((ng // 2,)), dma, dma,
            dma, dma, dma, dma, dma,
        ],
        compiler_params=pltpu.CompilerParams(
            collective_id=0, has_side_effects=True, vmem_limit_bytes=56 * 1024 * 1024
        ),
        cost_estimate=pl.CostEstimate(flops=5 * 10**9, bytes_accessed=5 * 10**6, transcendentals=4096),
        name="scores",
    )(
        queries[0].reshape(COLS, width),
        positives[0].reshape(Q * LANES, width),
        memory[0],
        candidates[0],
        counts,
    )
    return out_b[None], out_m[None], out_l


def solution(mesh):
    in_specs = (
        P("group", "memory", None, None),
        P("group", "memory", None, None),
        P("group", "memory", None, None),
        P("group", "memory", None),
        P("group", "memory"),
    )
    out_specs = (P("group", "memory", None), P("group", "memory", None), P("group", "memory"))
    return jax.shard_map(body, mesh=mesh, in_specs=in_specs, out_specs=out_specs, check_vma=False)
```

```python
import functools
import math

import jax
import jax.numpy as jnp
from jax import lax
from jax.experimental import pallas as pl
from jax.experimental.pallas import tpu as pltpu
from jax.sharding import PartitionSpec as P

MESH = pl.DeviceIdType.MESH
F32 = jnp.float32
BF16 = jnp.bfloat16
I32 = jnp.int32
CAP = 24
Q = 8
TOK = 32
LIVE = 32
LANES = 128
COLS = Q * TOK
CHUNKS = 2


def iota(shape, axis):
    return lax.broadcasted_iota(I32, shape, axis)


def kernel(zs, side, q_hbm, pos_hbm, mem_hbm, cand_ref, cnt_ref, out_b, out_m, out_l,
           qv, posv, memv, zbuf, gbuf, asks, ids, best_b, best_m, row_out, row_in, tile_out, tile_in,
           load_sem, zr_sem, zl_sem, ar_sem, al_sem, id_sem, cls_sem, sib_sem, row_sem, tile_sem,
           zsend_sem, asend_sem, gsend_sem, row_send_sem, tile_send_sem):
    half = zs // 2
    plane = side * side
    ng = 2 * plane
    side_bits = side.bit_length() - 1
    rows_of = LANES // CHUNKS

    z = lax.axis_index("memory")
    g = lax.axis_index("group")
    core = g & 1
    px = (g >> 1) & (side - 1)
    py = g >> (1 + side_bits)
    sibling = g + 1 - 2 * core

    def source(k, c):
        a, b = k % side, k // side
        dx = a + c * (b - a)
        dy = b + c * (a - b)
        return (((py - dy) & (side - 1)) * side + ((px - dx) & (side - 1))) * 2 + c

    def target(a, b):
        dx = a + core * (b - a)
        dy = b + core * (a - b)
        return (((py + dy) & (side - 1)) * side + ((px + dx) & (side - 1))) * 2 + core

    def block_of(n):
        return source(n, core) if n < plane else source(n - plane, 1 - core)

    load_q = pltpu.make_async_copy(q_hbm, qv, load_sem.at[0])
    load_pos = pltpu.make_async_copy(pos_hbm, posv, load_sem.at[1])
    load_mem = pltpu.make_async_copy(mem_hbm, memv, load_sem.at[2])
    load_q.start()
    load_pos.start()
    load_mem.start()

    barrier = pltpu.get_barrier_semaphore()
    partners = [((z + o) & (zs - 1), g) for o in (1, -1, 2, -2)] + [(z, sibling)]
    for a in range(1, side):
        partners += [(z, target(a, 0)), (z, target(0, a))]
    for to in partners:
        pl.semaphore_signal(barrier, inc=1, device_id=to, device_id_type=MESH)

    load_q.wait()
    turned = qv[...].astype(F32).T.astype(BF16)
    zbuf[z] = turned
    gbuf[g] = turned

    pl.semaphore_wait(barrier, len(partners))

    def ring_copy(ref, send, recv, to):
        return pltpu.make_async_remote_copy(
            src_ref=ref, dst_ref=ref, send_sem=send, recv_sem=recv, device_id=(to, g), device_id_type=MESH
        )

    def right(d, c, step):
        block = (z - d + step) & (zs - 1)
        ref = zbuf.at[block, pl.ds(c * rows_of, rows_of)]
        return ring_copy(ref, zsend_sem, zr_sem.at[(d - 1) * CHUNKS + c], (z + max(step, 1)) & (zs - 1))

    def left(d, c, step):
        block = (z + d - step) & (zs - 1)
        ref = zbuf.at[block, pl.ds(c * rows_of, rows_of)]
        return ring_copy(ref, zsend_sem, zl_sem.at[(d - 1) * CHUNKS + c], (z - max(step, 1)) & (zs - 1))

    def right_ask(d, step):
        return ring_copy(asks.at[(z - d + step) & (zs - 1)], asend_sem, ar_sem.at[d - 1], (z + max(step, 1)) & (zs - 1))

    def left_ask(d, step):
        return ring_copy(asks.at[(z + d - step) & (zs - 1)], asend_sem, al_sem.at[d - 1], (z - max(step, 1)) & (zs - 1))

    def by_right(d, c):
        return d < half or (d == half and c < CHUNKS // 2)

    def by_left(d, c):
        return d < half or (d == half and c >= CHUNKS // 2)

    def pass_on(d, c):
        for step in (2, 1):
            if by_right(d + step, c):
                right(d + step, c, step).start()
            if by_left(d + step, c):
                left(d + step, c, step).start()

    def pass_asks_right(d):
        for step in (2, 1):
            if d + step <= half:
                right_ask(d + step, step).start()

    def pass_asks_left(d):
        for step in (2, 1):
            if d + step < half:
                left_ask(d + step, step).start()

    def g_copy(block, sem, to):
        ref = gbuf.at[block]
        return pltpu.make_async_remote_copy(
            src_ref=ref, dst_ref=ref, send_sem=gsend_sem, recv_sem=sem,
            device_id=(z, to), device_id_type=MESH,
        )

    def asker_of(n):
        d = (n + 1) // 2
        return (z - d if n % 2 else z + d) & (zs - 1)

    def load_ids(n):
        return pltpu.make_async_copy(asks.at[asker_of(n), z >> 1], ids.at[n], id_sem.at[n])

    for c in range(CHUNKS):
        pass_on(0, c)
    for a in range(1, side):
        g_copy(g, cls_sem.at[a], target(a, 0)).start()
    g_copy(g, sib_sem.at[0], sibling).start()
    for b in range(1, side):
        g_copy(g, cls_sem.at[b * side], target(0, b)).start()
    lane = iota((1, LANES), 1)
    cand = jnp.concatenate([cand_ref[...], jnp.zeros((Q, LANES - cand_ref.shape[1]), I32)], axis=1)
    parts, limits = [], []
    for h in range(2):
        flat = jnp.zeros((1, LANES), I32)
        limit = jnp.zeros((1, LANES), I32)
        for j in range(4):
            row = cand[4 * h + j : 4 * h + j + 1]
            if j:
                row = pltpu.roll(row, j * LIVE, 1)
            flat = jnp.where(lane >> 5 == j, row, flat)
            limit = jnp.where(lane >> 5 == j, cnt_ref[0, 4 * h + j], limit)
        parts.append(flat)
        limits.append(limit)
    flat = jnp.concatenate(parts, axis=1)
    limit = jnp.concatenate(limits, axis=1)
    slot = iota((1, COLS), 1)
    live = (slot & (LIVE - 1)) < limit
    owner = jnp.where(live, flat >> 7, -1)
    local = (flat & (LANES - 1)).astype(F32)
    query = (slot >> 5).astype(F32)
    onehot = jnp.where(iota((zs, COLS), 0) == owner, 1.0, 0.0).astype(F32)
    upper = jnp.where(iota((COLS, COLS), 0) < iota((COLS, COLS), 1), 1.0, 0.0).astype(BF16)
    before = jnp.dot(onehot.astype(BF16), upper, preferred_element_type=F32)
    rank = jnp.sum(onehot * before, axis=0, keepdims=True)
    place = iota((LANES, COLS), 0).astype(F32) == rank
    both = jnp.concatenate([onehot * local, onehot * query], axis=0).astype(BF16)
    table = lax.dot_general(
        both, jnp.where(place, 1.0, 0.0).astype(BF16), (((1,), (1,)), ((), ())), preferred_element_type=F32
    )
    code = (table[:zs] + 128.0 * table[zs:]).astype(I32)
    for o in range(zs // 2):
        asks[z, o] = code[2 * o : 2 * o + 1] + pltpu.roll(code[2 * o + 1 : 2 * o + 2], 64, 1)

    pass_asks_right(0)
    pass_asks_left(0)
    load_ids(0).start()

    def best(passages, tokens):
        r = jnp.dot(passages, tokens, preferred_element_type=F32)
        return jnp.max(r.reshape(passages.shape[0] // LANES, LANES, COLS), axis=1)

    lane8 = iota((8, LANES), 1)

    def batch_unit(n):
        best_b[n] = best(posv[...], gbuf[block_of(n)])

    def batch_finish(ns):
        for n in ns:
            x0, x1 = best_b[n, :, :LANES], best_b[n, :, LANES:]
            x0 = x0 + pltpu.roll(x0, LANES - 16, 1)
            x1 = x1 + pltpu.roll(x1, LANES - 16, 1)
            x = jnp.where((lane8 & 31) < 16, x0, pltpu.roll(x1, 16, 1))
            for s in (8, 4, 2, 1):
                x = x + pltpu.roll(x, LANES - s, 1)
            if n == 0:
                tile_in[g] = x
            else:
                tile_out[n] = x

    def batch_send(ns):
        for n in ns:
            if n:
                pltpu.make_async_remote_copy(
                    src_ref=tile_out.at[n], dst_ref=tile_in.at[g], send_sem=tile_send_sem, recv_sem=tile_sem,
                    device_id=(z, block_of(n)), device_id_type=MESH,
                ).start()

    diag = iota((CAP, LANES), 0) == iota((CAP, LANES), 1)
    col_query = iota((CAP, COLS), 1) >> 5
    upper_half = (z & 1) * 64

    def memory_unit(n, part):
        first = part * 8
        passages = jnp.concatenate(
            [memv[ids[n, 0, upper_half + first + j] & (LANES - 1)] for j in range(8)], axis=0
        )
        best_m[n, pl.ds(first, 8)] = best(passages, zbuf[asker_of(n)])

    def memory_finish(ns):
        for n in ns:
            row = asks[asker_of(n), z >> 1].astype(F32)
            row = jnp.where(upper_half > 0, pltpu.roll(row, 64, 1), row)
            asked = jnp.sum(jnp.where(diag, row, 0.0), axis=1, keepdims=True).astype(I32) >> 7
            s = jnp.sum(jnp.where(col_query == asked, best_m[n], 0.0), axis=1, keepdims=True)
            scores = jnp.sum(jnp.where(diag, s, 0.0), axis=0, keepdims=True)
            if n == 0:
                row_in[z] = scores
            else:
                row_out[n] = scores

    def memory_send(ns):
        for n in ns:
            if n:
                pltpu.make_async_remote_copy(
                    src_ref=row_out.at[n], dst_ref=row_in.at[z], send_sem=row_send_sem, recv_sem=row_sem,
                    device_id=(asker_of(n), g), device_id_type=MESH,
                ).start()

    turns = CHUNKS * half
    moves = [[] for _ in range(turns + 5)]
    sums = [[] for _ in range(turns + 5)]

    def z_turn(d, c):
        def run():
            if c == 0:
                right_ask(d, 0).wait_recv()
                if d % 2 == 0:
                    pass_asks_right(d)
                if d < half:
                    left_ask(d, 0).wait_recv()
                    if d % 2 == 0:
                        pass_asks_left(d)
                    load_ids(2 * d).start()
                load_ids(2 * d - 1).start()
            if by_right(d, c):
                right(d, c, 0).wait_recv()
            if by_left(d, c):
                left(d, c, 0).wait_recv()
            if d % 2 == 0:
                pass_on(d, c)

        return run

    line = []
    for d in range(2, half, 2):
        for c in range(CHUNKS):
            line += [(d, c), (d - 1, c)]
    line += [(half - 1, c) for c in range(CHUNKS)] + [(half, c) for c in range(CHUNKS)]
    for t, (d, c) in enumerate(line):
        moves[t].append(z_turn(d, c))

    def cls_arrives(k):
        def run():
            block = source(k, core)
            g_copy(block, cls_sem.at[k], sibling).wait_recv()
            if k < side:
                for b in range(1, side):
                    g_copy(block, cls_sem.at[b * side + k], target(0, b)).start()
            g_copy(block, sib_sem.at[k], sibling).start()

        return run

    def sib_arrives(k):
        return lambda: g_copy(source(k, 1 - core), sib_sem.at[k], sibling).wait_recv()

    order = [(0, 0)]
    arrival = [0] * plane
    for k in range(1, plane):
        t = 2 if k < side else min(turns - 1, 2 * side + 5 * (k - side) // 4)
        moves[t].append(cls_arrives(k))
        arrival[k] = t
        order.append((max(t, min(turns - 1, 2 * k - 2)), k))
    for k in range(plane):
        t = min(turns, max(2 * k + 1, arrival[k] + 2))
        moves[t].append(sib_arrives(k))
        order.append((t, plane + k))
    order.sort()
    first = 0
    while first < ng:
        ns = [n for _, n in order[first : first + 8]]
        last_turn = order[min(ng, first + 8) - 1][0]
        sums[last_turn + 1].append(functools.partial(batch_finish, ns))
        moves[last_turn + 2].append(functools.partial(batch_send, ns))
        first += 8
    for t, n in order:
        sums[t].append(functools.partial(batch_unit, n))

    def ids_arrive(ns):
        for n in ns:
            load_ids(n).wait()

    def mem_start():
        load_mem.wait()
        load_pos.wait()
        ids_arrive([0])

    moves[0].insert(0, mem_start)
    for part in range(3):
        sums[0].append(functools.partial(memory_unit, 0, part))
    sums[1].append(functools.partial(memory_finish, [0]))
    for d in range(1, half + 1):
        ns = [2 * d - 1, 2 * d] if d < half else [2 * d - 1]
        start = line.index((d, CHUNKS - 1))
        moves[start].append(functools.partial(ids_arrive, ns))
        units = [(n, part) for n in ns for part in range(3)]
        spread = 1 if d == half else CHUNKS - 1
        if d % 2 and d + 1 < half:
            start += spread
        for i, (n, part) in enumerate(units):
            sums[start + i * spread // len(units)].append(functools.partial(memory_unit, n, part))
        sums[start + spread].append(functools.partial(memory_finish, ns))
        moves[start + spread + 1].append(functools.partial(memory_send, ns))

    for t in range(turns + 5):
        for move in moves[t]:
            move()
        for work in sums[t]:
            work()

    pltpu.make_async_copy(tile_in.at[pl.ds(0, ng - 1)], tile_in.at[pl.ds(0, ng - 1)], tile_sem).wait()
    turned_scores = tile_in[...].reshape(ng * 8, LANES).T
    order = [0, 32, 64, 96, 16, 48, 80, 112]
    rows = jnp.concatenate([turned_scores[o : o + 1] for o in order], axis=0)
    out_b[...] = rows
    most = jnp.max(rows, axis=1, keepdims=True)
    mine = iota(rows.shape, 1) == g * Q + iota(rows.shape, 0)
    own = jnp.sum(jnp.where(mine, rows, 0.0), axis=1, keepdims=True)
    gathered = jnp.sum(jnp.exp(rows - most), axis=1, keepdims=True)

    pltpu.make_async_copy(row_in.at[pl.ds(0, zs - 1)], row_in.at[pl.ds(0, zs - 1)], row_sem).wait()
    got = jnp.concatenate([row_in[o] for o in range(zs)], axis=0)
    spread = lax.dot_general(
        got, onehot, (((0,), (0,)), ((), ())), preferred_element_type=F32, precision=lax.Precision.HIGHEST
    )
    picked = jnp.sum(jnp.where(place, spread, 0.0), axis=0, keepdims=True)
    sub8 = iota((Q, LANES), 0)
    scores = jnp.zeros((Q, LANES), F32)
    count = jnp.zeros((Q, LANES), I32)
    for q in range(Q):
        h, j = q // 4, q % 4
        row = picked[:, h * LANES : (h + 1) * LANES]
        if j:
            row = pltpu.roll(row, LANES - j * LIVE, 1)
        scores = jnp.where(sub8 == q, row, scores)
        count = jnp.where(sub8 == q, cnt_ref[0, q], count)
    valid = lane8 < count
    scores = jnp.where(valid, scores, 0.0)
    out_m[...] = scores[:, : out_m.shape[1]]

    top = jnp.maximum(most, jnp.max(jnp.where(valid, scores, -jnp.inf), axis=1, keepdims=True))
    total = gathered * jnp.exp(most - top) + jnp.sum(
        jnp.where(valid, jnp.exp(scores - top), 0.0), axis=1, keepdims=True
    )
    loss = top + jnp.log(total) - own
    spread_loss = jnp.where(lane8 == sub8, loss, 0.0)
    out_l[...] = jnp.sum(spread_loss, axis=0, keepdims=True)[:, :Q]

    items = zs - 1
    pltpu.make_async_copy(zbuf.at[pl.ds(0, items)], zbuf.at[pl.ds(0, items)], zsend_sem).wait()
    pltpu.make_async_copy(gbuf.at[pl.ds(0, ng - 1)], gbuf.at[pl.ds(0, ng - 1)], gsend_sem).wait()
    pltpu.make_async_copy(asks.at[pl.ds(0, items)], asks.at[pl.ds(0, items)], asend_sem).wait()
    pltpu.make_async_copy(row_in.at[pl.ds(0, items)], row_in.at[pl.ds(0, items)], row_send_sem).wait()
    pltpu.make_async_copy(tile_in.at[pl.ds(0, ng - 1)], tile_in.at[pl.ds(0, ng - 1)], tile_send_sem).wait()


def hand_over(in_b, in_m, in_l, out_b, out_m, out_l):
    out_b[...] = in_b[...]
    out_m[...] = in_m[...]
    out_l[...] = in_l[...]


def body(queries, positives, memory, candidates, counts):
    zs = lax.axis_size("memory")
    ng = lax.axis_size("group")
    side = math.isqrt(ng // 2)
    assert ng == 2 * side * side and zs == side * side
    width = queries.shape[3]
    p_local = memory.shape[1]
    any_space = pl.BlockSpec(memory_space=pltpu.HBM)
    vmem = pl.BlockSpec(memory_space=pltpu.VMEM)
    smem = pl.BlockSpec(memory_space=pltpu.SMEM)
    dma = pltpu.SemaphoreType.DMA
    slots = candidates.shape[2]
    out_b, out_m, out_l = pl.pallas_call(
        functools.partial(kernel, zs, side),
        out_shape=(
            jax.ShapeDtypeStruct((Q, ng * Q), F32),
            jax.ShapeDtypeStruct((Q, slots), F32),
            jax.ShapeDtypeStruct((1, Q), F32),
        ),
        in_specs=[any_space, any_space, any_space, vmem, smem],
        out_specs=(vmem, vmem, vmem),
        scratch_shapes=[
            pltpu.VMEM((COLS, width), BF16),
            pltpu.VMEM((Q * LANES, width), BF16),
            pltpu.VMEM((p_local, LANES, width), BF16),
            pltpu.VMEM((zs, width, COLS), BF16),
            pltpu.VMEM((ng, width, COLS), BF16),
            pltpu.VMEM((zs, zs // 2, 1, LANES), I32),
            pltpu.SMEM((zs, 1, LANES), I32),
            pltpu.VMEM((ng, 8, COLS), F32),
            pltpu.VMEM((zs, CAP, COLS), F32),
            pltpu.VMEM((zs, 1, LANES), F32),
            pltpu.VMEM((zs, 1, LANES), F32),
            pltpu.VMEM((ng, 8, LANES), F32),
            pltpu.VMEM((ng, 8, LANES), F32),
            dma((3,)), dma((zs // 2 * CHUNKS,)), dma((zs // 2 * CHUNKS,)), dma((zs // 2,)), dma((zs // 2,)),
            dma((zs,)), dma((ng // 2,)), dma((ng // 2,)), dma, dma,
            dma, dma, dma, dma, dma,
        ],
        compiler_params=pltpu.CompilerParams(
            collective_id=0, has_side_effects=True, vmem_limit_bytes=56 * 1024 * 1024
        ),
        cost_estimate=pl.CostEstimate(flops=5 * 10**9, bytes_accessed=5 * 10**6, transcendentals=4096),
        name="scores",
    )(
        queries[0].reshape(COLS, width),
        positives[0].reshape(Q * LANES, width),
        memory[0],
        candidates[0],
        counts,
    )
    out_b, out_m, out_l = pl.pallas_call(
        hand_over,
        out_shape=tuple(jax.ShapeDtypeStruct(x.shape, F32) for x in (out_b, out_m, out_l)),
        in_specs=[vmem, vmem, vmem],
        out_specs=(vmem, vmem, vmem),
        name="results",
    )(out_b, out_m, out_l)
    return out_b[None], out_m[None], out_l


def solution(mesh):
    in_specs = (
        P("group", "memory", None, None),
        P("group", "memory", None, None),
        P("group", "memory", None, None),
        P("group", "memory", None),
        P("group", "memory"),
    )
    out_specs = (P("group", "memory", None), P("group", "memory", None), P("group", "memory"))
    return jax.shard_map(body, mesh=mesh, in_specs=in_specs, out_specs=out_specs, check_vma=False)
```

```python
import functools
import math

import jax
import jax.numpy as jnp
from jax import lax
from jax.experimental import pallas as pl
from jax.experimental.pallas import tpu as pltpu
from jax.sharding import PartitionSpec as P

MESH = pl.DeviceIdType.MESH
F32 = jnp.float32
BF16 = jnp.bfloat16
I32 = jnp.int32
CAP = 24
Q = 8
TOK = 32
LIVE = 32
LANES = 128
COLS = Q * TOK
CHUNKS = 2
BESIDE = 12


def iota(shape, axis):
    return lax.broadcasted_iota(I32, shape, axis)


def kernel(zs, side, q_hbm, pos_hbm, mem_hbm, cand_ref, cnt_ref, out_b, out_m, out_l,
           qv, posv, memv, zbuf, gbuf, asks, ids, best_b, best_m, row_out, row_in, tile_out, tile_in,
           load_sem, zr_sem, zl_sem, ar_sem, al_sem, id_sem, cls_sem, sib_sem, row_sem, tile_sem,
           zsend_sem, asend_sem, gsend_sem, row_send_sem, tile_send_sem):
    half = zs // 2
    plane = side * side
    ng = 2 * plane
    side_bits = side.bit_length() - 1
    rows_of = LANES // CHUNKS

    z = lax.axis_index("memory")
    g = lax.axis_index("group")
    core = g & 1
    px = (g >> 1) & (side - 1)
    py = g >> (1 + side_bits)
    sibling = g + 1 - 2 * core

    def source(k, c):
        a, b = k % side, k // side
        dx = a + c * (b - a)
        dy = b + c * (a - b)
        return (((py - dy) & (side - 1)) * side + ((px - dx) & (side - 1))) * 2 + c

    def target(a, b):
        dx = a + core * (b - a)
        dy = b + core * (a - b)
        return (((py + dy) & (side - 1)) * side + ((px + dx) & (side - 1))) * 2 + core

    def block_of(n):
        return source(n, core) if n < plane else source(n - plane, 1 - core)

    load_q = pltpu.make_async_copy(q_hbm, qv, load_sem.at[0])
    load_pos = pltpu.make_async_copy(pos_hbm, posv, load_sem.at[1])
    load_mem = pltpu.make_async_copy(mem_hbm, memv, load_sem.at[2])
    load_q.start()
    load_pos.start()
    load_mem.start()

    barrier = pltpu.get_barrier_semaphore()
    partners = [((z + o) & (zs - 1), g) for o in (1, -1, 2, -2)] + [(z, sibling)]
    for a in range(1, side):
        partners += [(z, target(a, 0)), (z, target(0, a))]
    for to in partners:
        pl.semaphore_signal(barrier, inc=1, device_id=to, device_id_type=MESH)

    load_q.wait()
    turned = qv[...].astype(F32).T.astype(BF16)
    zbuf[z] = turned
    gbuf[g] = turned

    pl.semaphore_wait(barrier, len(partners))

    def ring_copy(ref, send, recv, to):
        return pltpu.make_async_remote_copy(
            src_ref=ref, dst_ref=ref, send_sem=send, recv_sem=recv, device_id=(to, g), device_id_type=MESH
        )

    def right(d, c, step):
        block = (z - d + step) & (zs - 1)
        ref = zbuf.at[block, pl.ds(c * rows_of, rows_of)]
        return ring_copy(ref, zsend_sem, zr_sem.at[(d - 1) * CHUNKS + c], (z + max(step, 1)) & (zs - 1))

    def left(d, c, step):
        block = (z + d - step) & (zs - 1)
        ref = zbuf.at[block, pl.ds(c * rows_of, rows_of)]
        return ring_copy(ref, zsend_sem, zl_sem.at[(d - 1) * CHUNKS + c], (z - max(step, 1)) & (zs - 1))

    def right_ask(d, step):
        return ring_copy(asks.at[(z - d + step) & (zs - 1)], asend_sem, ar_sem.at[d - 1], (z + max(step, 1)) & (zs - 1))

    def left_ask(d, step):
        return ring_copy(asks.at[(z + d - step) & (zs - 1)], asend_sem, al_sem.at[d - 1], (z - max(step, 1)) & (zs - 1))

    def by_right(d, c):
        return d < half or (d == half and c < CHUNKS // 2)

    def by_left(d, c):
        return d < half or (d == half and c >= CHUNKS // 2)

    def pass_on(d, c):
        for step in (2, 1):
            if by_right(d + step, c):
                right(d + step, c, step).start()
            if by_left(d + step, c):
                left(d + step, c, step).start()

    def pass_asks_right(d):
        for step in (2, 1):
            if d + step <= half:
                right_ask(d + step, step).start()

    def pass_asks_left(d):
        for step in (2, 1):
            if d + step < half:
                left_ask(d + step, step).start()

    def g_copy(block, sem, to):
        ref = gbuf.at[block]
        return pltpu.make_async_remote_copy(
            src_ref=ref, dst_ref=ref, send_sem=gsend_sem, recv_sem=sem,
            device_id=(z, to), device_id_type=MESH,
        )

    def asker_of(n):
        d = (n + 1) // 2
        return (z - d if n % 2 else z + d) & (zs - 1)

    def load_ids(n):
        return pltpu.make_async_copy(asks.at[asker_of(n), z >> 1], ids.at[n], id_sem.at[n])

    for c in range(CHUNKS):
        pass_on(0, c)
    for a in range(1, side):
        g_copy(g, cls_sem.at[a], target(a, 0)).start()
    g_copy(g, sib_sem.at[0], sibling).start()
    for b in range(1, side):
        g_copy(g, cls_sem.at[b * side], target(0, b)).start()
    lane = iota((1, LANES), 1)
    cand = jnp.concatenate([cand_ref[...], jnp.zeros((Q, LANES - cand_ref.shape[1]), I32)], axis=1)
    parts, limits = [], []
    for h in range(2):
        flat = jnp.zeros((1, LANES), I32)
        limit = jnp.zeros((1, LANES), I32)
        for j in range(4):
            row = cand[4 * h + j : 4 * h + j + 1]
            if j:
                row = pltpu.roll(row, j * LIVE, 1)
            flat = jnp.where(lane >> 5 == j, row, flat)
            limit = jnp.where(lane >> 5 == j, cnt_ref[0, 4 * h + j], limit)
        parts.append(flat)
        limits.append(limit)
    flat = jnp.concatenate(parts, axis=1)
    limit = jnp.concatenate(limits, axis=1)
    slot = iota((1, COLS), 1)
    live = (slot & (LIVE - 1)) < limit
    owner = jnp.where(live, flat >> 7, -1)
    local = (flat & (LANES - 1)).astype(F32)
    query = (slot >> 5).astype(F32)
    onehot = jnp.where(iota((zs, COLS), 0) == owner, 1.0, 0.0).astype(F32)
    upper = jnp.where(iota((COLS, COLS), 0) < iota((COLS, COLS), 1), 1.0, 0.0).astype(BF16)
    before = jnp.dot(onehot.astype(BF16), upper, preferred_element_type=F32)
    rank = jnp.sum(onehot * before, axis=0, keepdims=True)
    place = iota((LANES, COLS), 0).astype(F32) == rank
    both = jnp.concatenate([onehot * local, onehot * query], axis=0).astype(BF16)
    table = lax.dot_general(
        both, jnp.where(place, 1.0, 0.0).astype(BF16), (((1,), (1,)), ((), ())), preferred_element_type=F32
    )
    code = (table[:zs] + 128.0 * table[zs:]).astype(I32)
    for o in range(zs // 2):
        asks[z, o] = code[2 * o : 2 * o + 1] + pltpu.roll(code[2 * o + 1 : 2 * o + 2], 64, 1)

    pass_asks_right(0)
    pass_asks_left(0)
    load_ids(0).start()

    def best(passages, tokens):
        r = jnp.dot(passages, tokens, preferred_element_type=F32)
        return jnp.max(r.reshape(passages.shape[0] // LANES, LANES, COLS), axis=1)

    lane8 = iota((8, LANES), 1)

    def batch_unit(n):
        best_b[n] = best(posv[...], gbuf[block_of(n)])

    def batch_finish(ns):
        for n in ns:
            x0, x1 = best_b[n, :, :LANES], best_b[n, :, LANES:]
            x0 = x0 + pltpu.roll(x0, LANES - 16, 1)
            x1 = x1 + pltpu.roll(x1, LANES - 16, 1)
            x = jnp.where((lane8 & 31) < 16, x0, pltpu.roll(x1, 16, 1))
            for s in (8, 4, 2, 1):
                x = x + pltpu.roll(x, LANES - s, 1)
            if n == 0:
                tile_in[g] = x
            else:
                tile_out[n] = x

    def batch_send(ns):
        for n in ns:
            if n:
                pltpu.make_async_remote_copy(
                    src_ref=tile_out.at[n], dst_ref=tile_in.at[g], send_sem=tile_send_sem, recv_sem=tile_sem,
                    device_id=(z, block_of(n)), device_id_type=MESH,
                ).start()

    diag = iota((CAP, LANES), 0) == iota((CAP, LANES), 1)
    col_query = iota((CAP, COLS), 1) >> 5
    upper_half = (z & 1) * 64

    def memory_unit(n, part):
        first = part * 8
        passages = jnp.concatenate(
            [memv[ids[n, 0, upper_half + first + j] & (LANES - 1)] for j in range(8)], axis=0
        )
        best_m[n, pl.ds(first, 8)] = best(passages, zbuf[asker_of(n)])

    def memory_finish(ns):
        for n in ns:
            row = asks[asker_of(n), z >> 1].astype(F32)
            row = jnp.where(upper_half > 0, pltpu.roll(row, 64, 1), row)
            asked = jnp.sum(jnp.where(diag, row, 0.0), axis=1, keepdims=True).astype(I32) >> 7
            s = jnp.sum(jnp.where(col_query == asked, best_m[n], 0.0), axis=1, keepdims=True)
            scores = jnp.sum(jnp.where(diag, s, 0.0), axis=0, keepdims=True)
            if n == 0:
                row_in[z] = scores
            else:
                row_out[n] = scores

    def memory_send(ns):
        for n in ns:
            if n:
                pltpu.make_async_remote_copy(
                    src_ref=row_out.at[n], dst_ref=row_in.at[z], send_sem=row_send_sem, recv_sem=row_sem,
                    device_id=(asker_of(n), g), device_id_type=MESH,
                ).start()

    def first_far(turns):
        return turns // 4

    turns = CHUNKS * half
    moves = [[] for _ in range(turns + 5)]
    sums = [[] for _ in range(turns + 5)]

    def z_turn(d, c):
        def ask():
            right_ask(d, 0).wait_recv()
            if d % 2 == 0:
                pass_asks_right(d)
            if d < half:
                left_ask(d, 0).wait_recv()
                if d % 2 == 0:
                    pass_asks_left(d)
                load_ids(2 * d).start()
            load_ids(2 * d - 1).start()

        def run():
            if by_right(d, c):
                right(d, c, 0).wait_recv()
            if by_left(d, c):
                left(d, c, 0).wait_recv()
            if d % 2 == 0:
                pass_on(d, c)
            if c == (CHUNKS - 1 if d % 2 == 0 and d < half else 0):
                ask()

        return run

    line = []
    for d in range(2, half, 2):
        for c in range(CHUNKS):
            line += [(d, c)]
        line += [(d - 1, c) for c in range(CHUNKS)]
    line += [(half - 1, c) for c in range(CHUNKS)] + [(half, c) for c in range(CHUNKS)]
    for t, (d, c) in enumerate(line):
        moves[t].append(z_turn(d, c))

    def cls_arrives(k):
        def run():
            block = source(k, core)
            g_copy(block, cls_sem.at[k], sibling).wait_recv()
            if k < side:
                for b in range(1, side):
                    g_copy(block, cls_sem.at[b * side + k], target(0, b)).start()
            g_copy(block, sib_sem.at[k], sibling).start()

        return run

    def sib_arrives(k):
        return lambda: g_copy(source(k, 1 - core), sib_sem.at[k], sibling).wait_recv()

    order = [(0, 0)]
    for k in range(1, plane):
        t = min(2, turns - 1) if k < side else min(turns - 1, first_far(turns) + (turns - first_far(turns)) * (k - side) // plane)
        moves[t].append(cls_arrives(k))
        arrives = [t, min(turns - 1, t + turns // 8)]
        moves[arrives[1]].append(sib_arrives(k))
        for t, n in zip(arrives, (k, plane + k)):
            order.append((t if k < side + BESIDE else turns + 1, n))
    moves[1].append(sib_arrives(0))
    order.append((1, plane))
    order.sort()
    early = [(t, n) for t, n in order if t < turns]
    late = [n for t, n in order if t >= turns]
    for t, n in early:
        sums[t].append(functools.partial(batch_unit, n))
    for first in range(0, len(early), 8):
        ns = [n for _, n in early[first : first + 8]]
        t = early[first : first + 8][-1][0]
        sums[t + 1].append(functools.partial(batch_finish, ns))
        moves[t + 2].append(functools.partial(batch_send, ns))

    def ids_arrive(ns):
        for n in ns:
            load_ids(n).wait()

    def mem_start():
        load_mem.wait()
        load_pos.wait()
        ids_arrive([0])

    moves[0].insert(0, mem_start)
    for part in range(3):
        sums[0].append(functools.partial(memory_unit, 0, part))
    sums[1].append(functools.partial(memory_finish, [0]))
    for d in range(1, half + 1):
        ns = [2 * d - 1, 2 * d] if d < half else [2 * d - 1]
        start = line.index((d, CHUNKS - 1))
        if d % 2 == 0 and d < half:
            start += 1
        moves[start].append(functools.partial(ids_arrive, ns))
        units = [(n, part) for n in ns for part in range(3)]
        spread = 1
        for i, (n, part) in enumerate(units):
            sums[start + i * spread // len(units)].append(functools.partial(memory_unit, n, part))
        sums[start + spread].append(functools.partial(memory_finish, ns))
        moves[start + spread + 1].append(functools.partial(memory_send, ns))

    for t in range(turns + 5):
        for move in moves[t]:
            move()
        for work in sums[t]:
            work()

    for first in range(0, len(late), 8):
        ns = late[first : first + 8]
        for n in ns:
            batch_unit(n)
        batch_finish(ns)
        batch_send(ns)

    pltpu.make_async_copy(tile_in.at[pl.ds(0, ng - 1)], tile_in.at[pl.ds(0, ng - 1)], tile_sem).wait()
    turned_scores = tile_in[...].reshape(ng * 8, LANES).T
    order = [0, 32, 64, 96, 16, 48, 80, 112]
    rows = jnp.concatenate([turned_scores[o : o + 1] for o in order], axis=0)
    out_b[...] = rows
    most = jnp.max(rows, axis=1, keepdims=True)
    mine = iota(rows.shape, 1) == g * Q + iota(rows.shape, 0)
    own = jnp.sum(jnp.where(mine, rows, 0.0), axis=1, keepdims=True)
    gathered = jnp.sum(jnp.exp(rows - most), axis=1, keepdims=True)

    pltpu.make_async_copy(row_in.at[pl.ds(0, zs - 1)], row_in.at[pl.ds(0, zs - 1)], row_sem).wait()
    got = jnp.concatenate([row_in[o] for o in range(zs)], axis=0)
    spread = lax.dot_general(
        got, onehot, (((0,), (0,)), ((), ())), preferred_element_type=F32, precision=lax.Precision.HIGHEST
    )
    picked = jnp.sum(jnp.where(place, spread, 0.0), axis=0, keepdims=True)
    sub8 = iota((Q, LANES), 0)
    scores = jnp.zeros((Q, LANES), F32)
    count = jnp.zeros((Q, LANES), I32)
    for q in range(Q):
        h, j = q // 4, q % 4
        row = picked[:, h * LANES : (h + 1) * LANES]
        if j:
            row = pltpu.roll(row, LANES - j * LIVE, 1)
        scores = jnp.where(sub8 == q, row, scores)
        count = jnp.where(sub8 == q, cnt_ref[0, q], count)
    valid = lane8 < count
    scores = jnp.where(valid, scores, 0.0)
    out_m[...] = scores[:, : out_m.shape[1]]

    top = jnp.maximum(most, jnp.max(jnp.where(valid, scores, -jnp.inf), axis=1, keepdims=True))
    total = gathered * jnp.exp(most - top) + jnp.sum(
        jnp.where(valid, jnp.exp(scores - top), 0.0), axis=1, keepdims=True
    )
    loss = top + jnp.log(total) - own
    spread_loss = jnp.where(lane8 == sub8, loss, 0.0)
    out_l[...] = jnp.sum(spread_loss, axis=0, keepdims=True)[:, :Q]

    items = zs - 1
    pltpu.make_async_copy(zbuf.at[pl.ds(0, items)], zbuf.at[pl.ds(0, items)], zsend_sem).wait()
    pltpu.make_async_copy(gbuf.at[pl.ds(0, ng - 1)], gbuf.at[pl.ds(0, ng - 1)], gsend_sem).wait()
    pltpu.make_async_copy(asks.at[pl.ds(0, items)], asks.at[pl.ds(0, items)], asend_sem).wait()
    pltpu.make_async_copy(row_in.at[pl.ds(0, items)], row_in.at[pl.ds(0, items)], row_send_sem).wait()
    pltpu.make_async_copy(tile_in.at[pl.ds(0, ng - 1)], tile_in.at[pl.ds(0, ng - 1)], tile_send_sem).wait()


def hand_over(in_b, in_m, in_l, out_b, out_m, out_l):
    out_b[...] = in_b[...]
    out_m[...] = in_m[...]
    out_l[...] = in_l[...]


def body(queries, positives, memory, candidates, counts):
    zs = lax.axis_size("memory")
    ng = lax.axis_size("group")
    side = math.isqrt(ng // 2)
    assert ng == 2 * side * side and zs == side * side
    width = queries.shape[3]
    p_local = memory.shape[1]
    any_space = pl.BlockSpec(memory_space=pltpu.HBM)
    vmem = pl.BlockSpec(memory_space=pltpu.VMEM)
    smem = pl.BlockSpec(memory_space=pltpu.SMEM)
    dma = pltpu.SemaphoreType.DMA
    slots = candidates.shape[2]
    out_b, out_m, out_l = pl.pallas_call(
        functools.partial(kernel, zs, side),
        out_shape=(
            jax.ShapeDtypeStruct((Q, ng * Q), F32),
            jax.ShapeDtypeStruct((Q, slots), F32),
            jax.ShapeDtypeStruct((1, Q), F32),
        ),
        in_specs=[any_space, any_space, any_space, vmem, smem],
        out_specs=(vmem, vmem, vmem),
        scratch_shapes=[
            pltpu.VMEM((COLS, width), BF16),
            pltpu.VMEM((Q * LANES, width), BF16),
            pltpu.VMEM((p_local, LANES, width), BF16),
            pltpu.VMEM((zs, width, COLS), BF16),
            pltpu.VMEM((ng, width, COLS), BF16),
            pltpu.VMEM((zs, zs // 2, 1, LANES), I32),
            pltpu.SMEM((zs, 1, LANES), I32),
            pltpu.VMEM((ng, 8, COLS), F32),
            pltpu.VMEM((zs, CAP, COLS), F32),
            pltpu.VMEM((zs, 1, LANES), F32),
            pltpu.VMEM((zs, 1, LANES), F32),
            pltpu.VMEM((ng, 8, LANES), F32),
            pltpu.VMEM((ng, 8, LANES), F32),
            dma((3,)), dma((zs // 2 * CHUNKS,)), dma((zs // 2 * CHUNKS,)), dma((zs // 2,)), dma((zs // 2,)),
            dma((zs,)), dma((ng // 2,)), dma((ng // 2,)), dma, dma,
            dma, dma, dma, dma, dma,
        ],
        compiler_params=pltpu.CompilerParams(
            collective_id=0, has_side_effects=True, vmem_limit_bytes=56 * 1024 * 1024
        ),
        cost_estimate=pl.CostEstimate(flops=5 * 10**9, bytes_accessed=5 * 10**6, transcendentals=4096),
        name="scores",
    )(
        queries[0].reshape(COLS, width),
        positives[0].reshape(Q * LANES, width),
        memory[0],
        candidates[0],
        counts,
    )
    out_b, out_m, out_l = pl.pallas_call(
        hand_over,
        out_shape=tuple(jax.ShapeDtypeStruct(x.shape, F32) for x in (out_b, out_m, out_l)),
        in_specs=[vmem, vmem, vmem],
        out_specs=(vmem, vmem, vmem),
        name="results",
    )(out_b, out_m, out_l)
    return out_b[None], out_m[None], out_l


def solution(mesh):
    in_specs = (
        P("group", "memory", None, None),
        P("group", "memory", None, None),
        P("group", "memory", None, None),
        P("group", "memory", None),
        P("group", "memory"),
    )
    out_specs = (P("group", "memory", None), P("group", "memory", None), P("group", "memory"))
    return jax.shard_map(body, mesh=mesh, in_specs=in_specs, out_specs=out_specs, check_vma=False)
```
